256 devices in a mesh: pcol: 32 (over y, x, core), prow: 8 (over z).
Axes of the slice: x: 4, y: 4, z: 8, core: 2. Of those that a mesh axis runs over, the one named last changes fastest.
Arguments:
- matrix: float32 [8, 32, 48, 32768], P(None, 'pcol', None, 'prow'), may hold values from -6 to 6, as said below
- pivots: int32 [96], replicated, may hold values from 0 to 32767, as said below
Outputs:
- factored: float32 [8, 32, 48, 32768], P(None, 'pcol', None, 'prow')
The draws below stay inside these ranges and needn't reach their ends.
Inputs may be any that keep to these rules, and one draw needn't show every extreme that they name: pivots[j] lies between j and 32767; some entry equals 32767. `matrix`: after the interchanges, the top 2 * 48 x 2 * 48 block of B is diagonally dominant by rows: diagonal entries of magnitude 4 to 6, off-diagonal magnitudes in a row summing to at most 3.5.
All inputs are finite; a program needn't handle non-finite values.
Results may differ from the reference program's by a relative error of at most 0.0001.
Values sent between devices are 32-bit elements; how exact they have to be, the bound alone decides.
No kernel may reach another device: no remote copies, remote signals or barrier semaphores. Data moves between devices by JAX's collectives and lax.ppermute only.
A program may use at most 64 MiB of HBM per device.

```python
import jax
import jax.numpy as jnp
from jax import lax

NB = 48
KB = 8
M = 32768
NCOLS = 12288
N_PCOL = 32


def pivot_list(key):
    key = jax.random.fold_in(key, 11)
    first_key, second_key = jax.random.split(key)
    positions = jnp.arange(2 * NB, dtype=jnp.int32)
    picks = jax.random.randint(first_key, (2 * NB,), positions, M, dtype=jnp.int32)
    marked = jax.random.randint(second_key, (), 0, 2 * NB, dtype=jnp.int32)
    return jnp.where(positions == marked, M - 1, picks).astype(jnp.int32)


def compose_order(pivot_values, length):
    ordering = jnp.arange(length, dtype=jnp.int32)

    def advance(counter, current):
        target = pivot_values[counter]
        at_counter = current[counter]
        at_target = current[target]
        return current.at[counter].set(at_target).at[target].set(at_counter)
    return lax.fori_loop(0, pivot_values.shape[0], advance, ordering)


def draw_pivots(key, part):
    return pivot_list(key)


def draw_matrix(key, part):
    pivot_values = pivot_list(key)
    key = jax.random.fold_in(key, 3)
    key_bulk, key_off, key_sign, key_size = jax.random.split(key, 4)
    top_span = 2 * NB
    spread = 3.5 / (top_span - 1)
    bulk = jnp.clip(jax.random.normal(key_bulk, (NCOLS, M), jnp.float32), -6.0, 6.0)
    off_part = spread * jax.random.uniform(key_off, (top_span, top_span), jnp.float32, -1.0, 1.0)
    signs = jnp.where(jax.random.bernoulli(key_sign, 0.5, (top_span,)), 1.0, -1.0)
    sizes_diag = 4.0 + 2.0 * jax.random.uniform(key_size, (top_span,), jnp.float32)
    diagonal_mask = jnp.arange(top_span)[:, None] == jnp.arange(top_span)[None, :]
    square = jnp.where(diagonal_mask, (signs * sizes_diag)[:, None], off_part)
    bulk = bulk.at[:top_span, :top_span].set(square)
    ordering = compose_order(pivot_values, M)
    inverse = jnp.zeros((M,), jnp.int32).at[ordering].set(jnp.arange(M, dtype=jnp.int32))
    return jnp.take(bulk, inverse, axis=1).astype(jnp.float32).reshape(KB, N_PCOL, NB, M)


def setup_inputs(seed: int = 0) -> dict:
    key_list = jax.random.split(jax.random.key(seed), 3)
    matrix = draw_matrix(jax.random.fold_in(key_list[2], 71), 0)
    pivots = draw_pivots(jax.random.fold_in(key_list[2], 71), 0)
    return {"matrix": matrix, "pivots": pivots}


def compose(swap_targets, length):
    ordering = jnp.arange(length, dtype=jnp.int32)

    def advance(counter, current):
        target = swap_targets[counter]
        at_counter = current[counter]
        at_target = current[target]
        return current.at[counter].set(at_target).at[target].set(at_counter)

    return lax.fori_loop(0, swap_targets.shape[0], advance, ordering)


def sweep_lower(coeffs, rhs, unit_diag):
    extent = coeffs.shape[0]
    indices = jnp.arange(extent)

    def advance(counter, current):
        head = current[counter]
        if not unit_diag:
            head = head / coeffs[counter, counter]
        current = current.at[counter].set(head)
        column = jnp.where(indices > counter, coeffs[:, counter], 0.0)
        return current - column[:, None] * head[None, :]

    return lax.fori_loop(0, extent, advance, rhs)


def eliminate(square):
    extent = square.shape[0]
    indices = jnp.arange(extent)

    def advance(counter, current):
        pivot_row = current[counter]
        column = current[:, counter] / pivot_row[counter]
        beneath = indices > counter
        current = current - jnp.where(beneath, column, 0.0)[:, None] * jnp.where(beneath, pivot_row, 0.0)[None, :]
        return jnp.where(beneath[:, None] & (indices[None, :] == counter), column[:, None], current)

    return lax.fori_loop(0, extent, advance, square)


def reference(matrix, pivots):
    transposed = matrix.reshape(NCOLS, M)
    ordering = compose(pivots, M)
    transposed = jnp.take(transposed, ordering, axis=1)
    for panel_number in range(2):
        first_col = panel_number * NB
        last_col = first_col + NB
        factored = eliminate(transposed[first_col:last_col, first_col:last_col].T)
        upper_part = jnp.triu(factored)
        unit_lower = jnp.tril(factored, -1) + jnp.eye(NB, dtype=transposed.dtype)
        multipliers = sweep_lower(upper_part.T, transposed[first_col:last_col, last_col:], False)
        trailing = transposed[last_col:, first_col:]
        solved = sweep_lower(unit_lower, trailing[:, :NB].T, True)
        remainder = trailing[:, NB:] - jnp.dot(solved.T, multipliers, precision=lax.Precision.HIGHEST, preferred_element_type=jnp.float32)
        transposed = transposed.at[first_col:last_col, first_col:last_col].set(factored.T)
        transposed = transposed.at[first_col:last_col, last_col:].set(multipliers)
        transposed = transposed.at[last_col:, first_col:last_col].set(solved.T)
        transposed = transposed.at[last_col:, last_col:].set(remainder)
    return transposed.reshape(KB, N_PCOL, NB, M)
```

```python
import jax
import jax.numpy as jnp
from jax import lax
from jax.experimental import pallas as pl
from jax.experimental.pallas import tpu as pltpu
from jax.sharding import Mesh
from jax.sharding import PartitionSpec as P

HI = lax.Precision.HIGHEST
LANES = 128
F32 = jnp.float32
BF16 = jnp.bfloat16


def iota(shape, dim):
    return lax.broadcasted_iota(jnp.int32, shape, dim)


def vmem_spec():
    return pl.BlockSpec(memory_space=pltpu.VMEM)


def smem_spec():
    return pl.BlockSpec(memory_space=pltpu.SMEM)


def params(mib=48):
    return pltpu.CompilerParams(vmem_limit_bytes=mib * 1024 * 1024)


def cost(us):
    return pl.CostEstimate(flops=0, bytes_accessed=int(us * 3.5e6), transcendentals=0)


def pick_rows(wanted, base, rows, block, out, top):
    lanes = iota((block.shape[0], LANES), 1)

    def step(i, carry):
        local = wanted[i] - base

        @pl.when((local >= 0) & (local < rows))
        def _():
            start = pl.multiple_of((local // LANES) * LANES, LANES)
            shift = (i + LANES - local % LANES) % LANES
            moved = pltpu.roll(block[:, pl.ds(start, LANES)], shift, 1)
            out[...] = jnp.where(lanes == i, moved, out[...])

        return carry

    out[...] = jnp.zeros(out.shape, F32)
    lax.fori_loop(0, top, step, 0)


def start_kernel(top, pivots, base, panel, blocks, wanted, dest, current, goes, picked):
    rows = panel.shape[1]
    groups = blocks.shape[0]
    width = rows // groups

    def fill(j, carry):
        current[pivots[j]] = pivots[j]
        goes[j] = -1
        return carry

    def fill_top(j, carry):
        current[j] = j
        return carry

    def swap(j, carry):
        t = pivots[j]
        a = current[j]
        b = current[t]
        wanted[j] = b
        current[t] = a
        goes[jnp.minimum(b, top)] = -1
        goes[a] = jnp.where(t >= top, t, -1)
        return carry

    def emit(j, carry):
        dest[pl.ds(j, 1), :] = jnp.full((1, LANES), goes[j], jnp.int32)
        return carry

    lax.fori_loop(0, top, fill, 0, unroll=8)
    lax.fori_loop(0, top, fill_top, 0, unroll=8)
    lax.fori_loop(0, top, swap, 0, unroll=8)
    dest[...] = jnp.full(dest.shape, -1, jnp.int32)
    lax.fori_loop(0, top, emit, 0, unroll=8)
    pick_rows(wanted, base[0], rows, panel, picked, top)
    lanes = iota(picked.shape, 1)
    heads = jnp.where((base[0] == 0) & (lanes < top), panel[:, :LANES], 0.0)
    for g in range(groups):
        blocks[g, :, :width] = panel[:, g * width : (g + 1) * width]
        blocks[g, :, width : width + LANES] = picked[...]
        blocks[g, :, width + LANES :] = heads


def own_kernel(top, base, wanted, block, *refs):
    outs, picked = refs[:-1], refs[-1]
    depth = len(outs)
    rows = block.shape[1]
    part = block.shape[0] // depth
    pick_rows(wanted, base[0], rows, block, picked, top)
    place = base[0] // rows
    for k, out in enumerate(outs):
        at = pl.ds(pl.multiple_of(((place + k) % depth) * part, 8), part)
        out[:, :LANES] = picked[at, :]
        lanes = iota((part, LANES), 1)
        out[:, LANES:] = jnp.where((base[0] == 0) & (lanes < top), block[at, :LANES], 0.0)


def gather_kernel(top, arrived, *refs):
    pieces, (shares, packed) = refs[:-2], refs[-2:]
    width = shares.shape[2]
    share = arrived[0, :, :width]
    for g in range(shares.shape[0]):
        shares[g] = share
    total = pieces[0][...]
    for piece in pieces[1:]:
        total = total + piece[...]
    square = arrived[0, :, width : width + LANES]
    begin = arrived[0, :, width + LANES :]
    third = LANES - top
    tail = iota(square.shape, 1) >= top
    for n, body in enumerate((total[:, :LANES], total[:, LANES:], square)):
        moved = pltpu.roll(begin, top - n * third, 1)
        packed[:, n * LANES : (n + 1) * LANES] = jnp.where(tail, moved, body)


def heads_kernel(top, place, *refs):
    pieces, (heads, square) = refs[:-2], refs[-2:]
    depth = len(pieces)
    part = pieces[0].shape[0]
    third = LANES - top
    lanes = iota((part, LANES), 1)
    total = pieces[0][...]
    for piece in pieces[1:]:
        total = total + piece[...]
    square[:, :LANES] = jnp.where(lanes < top, total[:, 2 * LANES :], 0.0)
    begin = jnp.zeros((part, LANES), F32)
    for n in range(3):
        moved = pltpu.roll(total[:, n * LANES : (n + 1) * LANES], LANES - top + n * third, 1)
        begin = jnp.where((lanes >= n * third) & (lanes < (n + 1) * third), moved, begin)
    square[:, LANES:] = begin
    keep = iota((part, 2 * LANES), 1) % LANES < top
    for k, piece in enumerate(pieces):
        owner = (place[0] + depth - k) % depth
        at = pl.ds(pl.multiple_of(owner * part, 8), part)
        heads[at, :] = jnp.where(keep, piece[:, : 2 * LANES], 0.0)


def spread(tile, j):
    return jnp.broadcast_to(tile[:, j : j + 1], (8, LANES))


def spread_row(tile, i):
    return jnp.broadcast_to(tile[i : i + 1, :], (8, LANES))


def reciprocal(x):
    r = pl.reciprocal(x, approx=True)
    r = r * (2.0 - x * r)
    return r * (2.0 - x * r)


def factor_kernel(core, mine, other, factor, lower_inv, upper_inv, starts):
    half = mine.shape[0]
    extent = 2 * half
    first = core[0] == 0
    m = mine[...]
    o = other[...]
    lo = jnp.where(first, m, o)
    hi = jnp.where(first, o, m)
    starts[:half, :] = lo[:, LANES:]
    starts[half:extent, :] = hi[:, LANES:]
    rest = jnp.zeros((LANES - extent, LANES), F32)
    starts[extent:, :] = rest
    tiles = [lo[8 * t : 8 * t + 8, :LANES] for t in range(half // 8)]
    tiles += [hi[8 * t : 8 * t + 8, :LANES] for t in range(half // 8)]
    square = jnp.concatenate(tiles + [rest], axis=0)
    lanes = iota((8, LANES), 1)
    subs = iota((8, LANES), 0)
    ahead = 2
    window = [[spread(t, q) for t in tiles] for q in range(ahead)]
    for j in range(extent):
        tj, sj = j // 8, j % 8
        here = lanes == j
        right = lanes > j
        cols = window.pop(0)
        if j + ahead < extent:
            window.append([spread(t, j + ahead) for t in tiles])
        row = spread_row(tiles[tj], sj)
        recip = reciprocal(spread_row(cols[tj], sj))
        scaled = jnp.where(here, recip, row * recip)
        right_part = jnp.where(right, scaled, 0.0)
        factor[j : j + 1, :] = right_part[:1]
        for q, nxt in enumerate(window):
            gain = spread_row(nxt[tj], sj) * recip
            moved = []
            for t, (n, col) in enumerate(zip(nxt, cols)):
                after = n - col * gain
                if t == tj:
                    after = jnp.where(subs == sj, -gain, after)
                moved.append(after)
            window[q] = moved
        new = []
        for t, (tile, col) in enumerate(zip(tiles, cols)):
            if t < tj:
                new.append(tile - col * right_part)
                continue
            below = jnp.where(here, 0.0, tile) - col * scaled
            if t == tj:
                above = tile - col * right_part
                at = jnp.where(right, -scaled, scaled)
                below = jnp.where(subs < sj, above, jnp.where(subs == sj, at, below))
            new.append(below)
        tiles = new
    for t, tile in enumerate(tiles):
        rows = subs + 8 * t
        at = pl.ds(8 * t, 8)
        lower_inv[at, :] = jnp.where(
            lanes > rows, jnp.where(lanes < extent, tile, 0.0), jnp.where(lanes == rows, 1.0, 0.0)
        )
        upper_inv[at, :] = jnp.where(lanes <= rows, tile, 0.0)
    factor[extent:, :] = rest
    lower_inv[extent:, :] = rest
    upper_inv[extent:, :] = rest
    upper = jnp.dot(square, lower_inv[...], precision=HI, preferred_element_type=F32)
    for t in range(extent // 8):
        at = pl.ds(8 * t, 8)
        rows = subs + 8 * t
        factor[at, :] = jnp.where(lanes > rows, factor[at, :], upper[8 * t : 8 * t + 8])


def split(x):
    head = x.astype(BF16)
    return head, (x - head.astype(F32)).astype(BF16)


def update_kernel(
    top, flags, heads, factor, lower_inv, upper_inv, starts, dest, block, mine, other, out,
    lhs_a, lhs_b, lhs_c, top_out,
):
    step = pl.program_id(0)
    half = mine.shape[1]
    width = block.shape[1]
    core, root, base = flags[0], flags[1], flags[2]

    @pl.when(step == 0)
    def _():
        tops = heads[:, :LANES]
        solved = jnp.dot(tops, lower_inv[...], precision=HI, preferred_element_type=F32)
        weight = jnp.dot(solved, upper_inv[...], precision=HI, preferred_element_type=F32)
        own_inv = jnp.where(core == 0, upper_inv[:half, :], upper_inv[half : 2 * half, :])
        own_fac = jnp.where(core == 0, factor[:half, :], factor[half : 2 * half, :])
        begin = heads[:, LANES:]
        is_root = root == 1
        weight = jnp.concatenate(
            [jnp.where(is_root, -own_inv, weight[:half]), weight[half:]], axis=0
        )
        begin = jnp.concatenate([jnp.where(is_root, 0.0, begin[:half]), begin[half:]], axis=0)
        top_out[...] = jnp.concatenate(
            [jnp.where(is_root, own_fac, solved[:half]), solved[half:]], axis=0
        )
        moved = begin - jnp.dot(weight, starts[...], precision=HI, preferred_element_type=F32)
        w_hi, w_lo = split(-weight)
        z_hi = moved.astype(BF16)
        left = moved - z_hi.astype(F32)
        z_mid, z_lo = split(left)
        lhs_a[:, :LANES] = w_hi
        lhs_a[:, LANES:] = z_hi
        lhs_b[:, :LANES] = w_lo
        lhs_b[:, LANES:] = z_mid
        lhs_c[:, :LANES] = w_hi
        lhs_c[:, LANES:] = z_lo

    groups = mine.shape[0]
    for g in range(groups):
        w = width // groups
        cols = slice(g * w, (g + 1) * w)
        m, o = mine[g], other[g]
        panel = jnp.concatenate([jnp.where(core == 0, m, o), jnp.where(core == 0, o, m)], axis=0)
        where_to = jnp.concatenate([dest[...]] * (w // LANES), axis=1)
        place = base + step * width + g * w + iota((LANES, w), 1)
        hot = jnp.where(where_to == place, 1.0, 0.0)
        keep = 1.0 - jnp.sum(hot, axis=0, keepdims=True)
        p_hi, p_lo = split(panel * keep)
        hot = hot.astype(BF16)
        fill = jnp.zeros((LANES - 2 * half, w), BF16)
        rhs_a = jnp.concatenate([p_hi, fill, hot], axis=0)
        rhs_c = jnp.concatenate([p_lo, fill, hot], axis=0)
        acc = jnp.dot(lhs_a[...], rhs_a, preferred_element_type=F32)
        acc += jnp.dot(lhs_b[...], rhs_a, preferred_element_type=F32)
        acc += jnp.dot(lhs_c[...], rhs_c, preferred_element_type=F32)
        keep_root = jnp.where(root == 1, 0.0, keep)
        out[:half, cols] = block[:half, cols] * keep_root + acc[:half]
        out[half:, cols] = block[half:, cols] * keep + acc[half:]

    @pl.when((step == 0) & (base == 0))
    def _():
        lanes = iota((block.shape[0], LANES), 1)
        out[:, :LANES] = jnp.where(lanes < top, top_out[...], out[:, :LANES])


def on_device(matrix, pivots):
    blocks, _, half, rows = matrix.shape
    cols = blocks * half
    top = 2 * half
    plane = ("y", "x")
    chips = lax.axis_size("y") * lax.axis_size("x")
    depth = lax.axis_size("prow")
    width = rows // chips
    holdings = matrix.reshape(cols, rows)
    core = lax.axis_index("core").astype(jnp.int32)
    base = (lax.axis_index("prow") * rows).astype(jnp.int32)
    root = ((lax.axis_index("y") == 0) & (lax.axis_index("x") == 0)).astype(jnp.int32)
    base1 = base.reshape(1)
    swap = [(0, 1), (1, 0)]

    def around(step):
        return [(z, (z + step) % depth) for z in range(depth)]

    def call(kernel, name, us, out_shape, in_specs, out_specs, *args, **more):
        return pl.pallas_call(
            lambda *refs: kernel(top, *refs),
            out_shape=out_shape,
            in_specs=in_specs,
            out_specs=out_specs,
            compiler_params=params(),
            cost_estimate=cost(us),
            name=name,
            **more,
        )(*args)

    blocks16, wanted, dest = call(
        start_kernel,
        "start",
        5,
        (
            jax.ShapeDtypeStruct((chips, half, width + 2 * LANES), F32),
            jax.ShapeDtypeStruct((top,), jnp.int32),
            jax.ShapeDtypeStruct((LANES, LANES), jnp.int32),
        ),
        [smem_spec(), smem_spec(), pl.BlockSpec((half, rows), lambda i: (0, 0))],
        (vmem_spec(), smem_spec(), vmem_spec()),
        pivots,
        base1,
        holdings,
        grid=(1,),
        scratch_shapes=[
            pltpu.SMEM((rows * depth,), jnp.int32),
            pltpu.SMEM((top + 8,), jnp.int32),
            pltpu.VMEM((half, LANES), F32),
        ],
    )
    arrived = lax.all_to_all(blocks16, plane, 0, 0)
    piece = jax.ShapeDtypeStruct((cols // depth, 2 * LANES), F32)
    offered = call(
        own_kernel,
        "own",
        5,
        (piece,) * depth,
        [smem_spec(), smem_spec(), vmem_spec()],
        (vmem_spec(),) * depth,
        base1,
        wanted,
        holdings,
        scratch_shapes=[pltpu.VMEM((cols, LANES), F32)],
    )
    pieces = [offered[0]]
    pieces += [lax.ppermute(offered[k], "prow", around(k)) for k in range(1, depth)]
    shares, packed = call(
        gather_kernel,
        "gather",
        2,
        (
            jax.ShapeDtypeStruct((chips, half, width), F32),
            jax.ShapeDtypeStruct((half, 3 * LANES), F32),
        ),
        [pl.BlockSpec((1, half, width + 2 * LANES), lambda i: (0, 0, 0))]
        + [pl.BlockSpec(piece.shape, lambda i: (0, 0))] * depth,
        (vmem_spec(), vmem_spec()),
        arrived,
        *pieces,
        grid=(1,),
    )
    mine = lax.all_to_all(shares, plane, 0, 0)
    slices = [packed] + [lax.ppermute(packed, "prow", around(k)) for k in range(1, depth)]
    heads, square = call(
        heads_kernel,
        "heads",
        1,
        (
            jax.ShapeDtypeStruct((cols, 2 * LANES), F32),
            jax.ShapeDtypeStruct((half, 2 * LANES), F32),
        ),
        [smem_spec()] + [vmem_spec()] * depth,
        (vmem_spec(), vmem_spec()),
        base1 // rows,
        *slices,
    )
    square_other = lax.ppermute(square, "core", swap)
    mine, square_other = lax.optimization_barrier((mine, square_other))
    other = lax.ppermute(mine, "core", swap)
    small = jax.ShapeDtypeStruct((LANES, LANES), F32)
    factor, lower_inv, upper_inv, starts = pl.pallas_call(
        factor_kernel,
        out_shape=(small,) * 4,
        in_specs=[smem_spec(), vmem_spec(), vmem_spec()],
        out_specs=(vmem_spec(),) * 4,
        compiler_params=params(),
        cost_estimate=cost(9),
        name="factor",
    )(core.reshape(1), square, square_other)
    flags = jnp.stack([core, root, base])
    per_step = 4
    span = per_step * width
    whole = pl.BlockSpec((LANES, LANES), lambda i: (0, 0))
    parts = pl.BlockSpec((per_step, half, width), lambda i: (i, 0, 0))
    result = pl.pallas_call(
        lambda *refs: update_kernel(top, *refs),
        grid=(rows // span,),
        out_shape=jax.ShapeDtypeStruct((cols, rows), F32),
        in_specs=[
            smem_spec(),
            pl.BlockSpec((cols, 2 * LANES), lambda i: (0, 0)),
            whole,
            whole,
            whole,
            whole,
            whole,
            pl.BlockSpec((cols, span), lambda i: (0, i)),
            parts,
            parts,
        ],
        out_specs=pl.BlockSpec((cols, span), lambda i: (0, i)),
        scratch_shapes=[
            pltpu.VMEM((cols, 2 * LANES), BF16),
            pltpu.VMEM((cols, 2 * LANES), BF16),
            pltpu.VMEM((cols, 2 * LANES), BF16),
            pltpu.VMEM((cols, LANES), F32),
        ],
        compiler_params=params(),
        cost_estimate=cost(8),
        name="update",
    )(flags, heads, factor, lower_inv, upper_inv, starts, dest, holdings, mine, other)
    return result.reshape(matrix.shape)


def solution(mesh):
    fine = Mesh(mesh.devices.reshape(4, 4, 2, 8), ("y", "x", "core", "prow"))
    spec = P(None, ("y", "x", "core"), None, "prow")
    return jax.shard_map(
        on_device, mesh=fine, in_specs=(spec, P()), out_specs=spec, check_vma=False
    )
```

```python
import jax
import jax.numpy as jnp
from jax import lax
from jax.experimental import pallas as pl
from jax.experimental.pallas import tpu as pltpu
from jax.sharding import Mesh
from jax.sharding import PartitionSpec as P

HI = lax.Precision.HIGHEST
LANES = 128
F32 = jnp.float32
BF16 = jnp.bfloat16


def iota(shape, dim):
    return lax.broadcasted_iota(jnp.int32, shape, dim)


def vmem_spec():
    return pl.BlockSpec(memory_space=pltpu.VMEM)


def smem_spec():
    return pl.BlockSpec(memory_space=pltpu.SMEM)


def params(mib=48):
    return pltpu.CompilerParams(vmem_limit_bytes=mib * 1024 * 1024)


def cost(us):
    return pl.CostEstimate(flops=0, bytes_accessed=int(us * 3.5e6), transcendentals=0)


def pick_rows(wanted, owned, base, block, out):
    lanes = iota((block.shape[0], LANES), 1)

    def step(n, carry):
        i = owned[n]
        local = wanted[i] - base

        @pl.when((local >= 0) & (local < block.shape[1]))
        def _():
            start = pl.multiple_of((local // LANES) * LANES, LANES)
            shift = (i + LANES - local % LANES) % LANES
            moved = pltpu.roll(block[:, pl.ds(start, LANES)], shift, 1)
            out[:, :LANES] = jnp.where(lanes == i, moved, out[:, :LANES])

        return carry

    lax.fori_loop(0, owned[owned.shape[0] - 8], step, 0)


def start_kernel(top, pivots, base, panel, *refs):
    sends, (wanted, owned, dest, current, goes, picked) = refs[:-6], refs[-6:]
    rows = panel.shape[1]
    span = len(sends)
    width = sends[0].shape[2]

    def fill(j, carry):
        current[pivots[j]] = pivots[j]
        goes[j] = -1
        return carry

    def fill_top(j, carry):
        current[j] = j
        return carry

    def swap(j, carry):
        t = pivots[j]
        a = current[j]
        b = current[t]
        wanted[j] = b
        current[t] = a
        goes[jnp.minimum(b, top)] = -1
        goes[a] = jnp.where(t >= top, t, -1)
        owned[carry] = j
        local = b - base[0]
        return carry + ((local >= 0) & (local < rows)).astype(jnp.int32)

    def emit(j, carry):
        dest[pl.ds(j, 1), :] = jnp.full((1, LANES), goes[j], jnp.int32)
        return carry

    lax.fori_loop(0, top, fill, 0, unroll=8)
    lax.fori_loop(0, top, fill_top, 0, unroll=8)
    owned[top] = lax.fori_loop(0, top, swap, 0, unroll=8)
    dest[...] = jnp.full(dest.shape, -1, jnp.int32)
    lax.fori_loop(0, top, emit, 0, unroll=8)
    picked[...] = jnp.zeros(picked.shape, F32)
    pick_rows(wanted, owned, base[0], panel, picked)
    lanes = iota(picked.shape, 1)
    heads = jnp.where((base[0] == 0) & (lanes < top), panel[:, :LANES], 0.0)
    for x, send in enumerate(sends):
        high = send.shape[0] - 1
        for y in range(high):
            g = y * span + x
            send[y] = panel[:, g * width : (g + 1) * width]
        send[high, :, :LANES] = picked[...]
        send[high, :, LANES:] = heads


def relay_kernel(top, root, kept, *refs):
    del top
    others, out = refs[:-1], refs[-1]
    for n in range(out.shape[0]):
        total = jnp.where(root[0] == 1, kept[n], 0.0)
        for other in others:
            total = total + other[n]
        out[n] = total


def own_kernel(top, base, wanted, owned, block, out):
    step = pl.program_id(0)

    @pl.when(step == 0)
    def _():
        lanes = iota((block.shape[0], LANES), 1)
        out[:, :LANES] = jnp.zeros(lanes.shape, F32)
        out[:, LANES:] = jnp.where((base[0] == 0) & (lanes < top), block[:, :LANES], 0.0)

    pick_rows(wanted, owned, base[0] + step * block.shape[1], block, out)


def arrive_kernel(top, *refs):
    del top
    arrivals, (share, square) = refs[:-2], refs[-2:]
    count = share.shape[0]
    for n in range(count + 1):
        total = arrivals[0][n]
        for arrival in arrivals[1:]:
            total = total + arrival[n]
        if n < count:
            share[n] = total
        else:
            square[...] = total


def order_kernel(top, place, *refs):
    del top
    pieces, out = refs[:-1], refs[-1]
    span = len(pieces)
    for k, piece in enumerate(pieces):
        owner = (place[0] + span - k) % span
        for n in range(piece.shape[0]):
            out[n * span + owner] = piece[n]


def gather_kernel(top, pieces, panel_top, packed):
    depth = pieces.shape[0]
    square, begin = panel_top[:, :LANES], panel_top[:, LANES:]
    total = pieces[0]
    for z in range(1, depth):
        total = total + pieces[z]
    third = LANES - top
    tail = iota(square.shape, 1) >= top
    for n, body in enumerate((total[:, :LANES], total[:, LANES:], square)):
        moved = pltpu.roll(begin, top - n * third, 1)
        value = jnp.where(tail, moved, body)
        for z in range(depth):
            packed[z, :, n * LANES : (n + 1) * LANES] = value


def heads_kernel(top, pieces, heads, square):
    depth, part, _ = pieces.shape
    third = LANES - top
    lanes = iota((part, LANES), 1)
    total = pieces[0]
    for z in range(1, depth):
        total = total + pieces[z]
    square[:, :LANES] = jnp.where(lanes < top, total[:, 2 * LANES :], 0.0)
    begin = jnp.zeros((part, LANES), F32)
    for n in range(3):
        moved = pltpu.roll(total[:, n * LANES : (n + 1) * LANES], LANES - top + n * third, 1)
        begin = jnp.where((lanes >= n * third) & (lanes < (n + 1) * third), moved, begin)
    square[:, LANES:] = begin
    keep = iota((part, 2 * LANES), 1) % LANES < top
    for z in range(depth):
        heads[z * part : (z + 1) * part, :] = jnp.where(keep, pieces[z, :, : 2 * LANES], 0.0)


def spread(tile, j):
    return jnp.broadcast_to(tile[:, j : j + 1], (8, LANES))


def spread_row(tile, i):
    return jnp.broadcast_to(tile[i : i + 1, :], (8, LANES))


def reciprocal(x):
    r = pl.reciprocal(x, approx=True)
    r = r * (2.0 - x * r)
    return r * (2.0 - x * r)


def factor_kernel(core, mine, other, factor, lower_inv, upper_inv, starts):
    half = mine.shape[0]
    extent = 2 * half
    first = core[0] == 0
    m = mine[...]
    o = other[...]
    lo = jnp.where(first, m, o)
    hi = jnp.where(first, o, m)
    starts[:half, :] = lo[:, LANES:]
    starts[half:extent, :] = hi[:, LANES:]
    rest = jnp.zeros((LANES - extent, LANES), F32)
    starts[extent:, :] = rest
    tiles = [lo[8 * t : 8 * t + 8, :LANES] for t in range(half // 8)]
    tiles += [hi[8 * t : 8 * t + 8, :LANES] for t in range(half // 8)]
    square = jnp.concatenate(tiles + [rest], axis=0)
    lanes = iota((8, LANES), 1)
    subs = iota((8, LANES), 0)
    ahead = 2
    window = [[spread(t, q) for t in tiles] for q in range(ahead)]
    for j in range(extent):
        tj, sj = j // 8, j % 8
        here = lanes == j
        right = lanes > j
        cols = window.pop(0)
        if j + ahead < extent:
            window.append([spread(t, j + ahead) for t in tiles])
        row = spread_row(tiles[tj], sj)
        recip = reciprocal(spread_row(cols[tj], sj))
        scaled = jnp.where(here, recip, row * recip)
        right_part = jnp.where(right, scaled, 0.0)
        factor[j : j + 1, :] = right_part[:1]
        for q, nxt in enumerate(window):
            gain = spread_row(nxt[tj], sj) * recip
            moved = []
            for t, (n, col) in enumerate(zip(nxt, cols)):
                after = n - col * gain
                if t == tj:
                    after = jnp.where(subs == sj, -gain, after)
                moved.append(after)
            window[q] = moved
        new = []
        for t, (tile, col) in enumerate(zip(tiles, cols)):
            if t < tj:
                new.append(tile - col * right_part)
                continue
            below = jnp.where(here, 0.0, tile) - col * scaled
            if t == tj:
                above = tile - col * right_part
                at = jnp.where(right, -scaled, scaled)
                below = jnp.where(subs < sj, above, jnp.where(subs == sj, at, below))
            new.append(below)
        tiles = new
    for t, tile in enumerate(tiles):
        rows = subs + 8 * t
        at = pl.ds(8 * t, 8)
        lower_inv[at, :] = jnp.where(
            lanes > rows, jnp.where(lanes < extent, tile, 0.0), jnp.where(lanes == rows, 1.0, 0.0)
        )
        upper_inv[at, :] = jnp.where(lanes <= rows, tile, 0.0)
    factor[extent:, :] = rest
    lower_inv[extent:, :] = rest
    upper_inv[extent:, :] = rest
    upper = jnp.dot(square, lower_inv[...], precision=HI, preferred_element_type=F32)
    for t in range(extent // 8):
        at = pl.ds(8 * t, 8)
        rows = subs + 8 * t
        factor[at, :] = jnp.where(lanes > rows, factor[at, :], upper[8 * t : 8 * t + 8])


def split(x):
    head = x.astype(BF16)
    return head, (x - head.astype(F32)).astype(BF16)


def update_kernel(
    top, flags, heads, factor, lower_inv, upper_inv, starts, dest, block, mine, other, out,
    lhs, top_out,
):
    step = pl.program_id(0)
    half = mine.shape[1]
    width = block.shape[1]
    core, root, base = flags[0], flags[1], flags[2]

    @pl.when(step == 0)
    def _():
        tops = heads[:, :LANES]
        solved = jnp.dot(tops, lower_inv[...], precision=HI, preferred_element_type=F32)
        weight = jnp.dot(solved, upper_inv[...], precision=HI, preferred_element_type=F32)
        own_inv = jnp.where(core == 0, upper_inv[:half, :], upper_inv[half : 2 * half, :])
        own_fac = jnp.where(core == 0, factor[:half, :], factor[half : 2 * half, :])
        begin = heads[:, LANES:]
        is_root = root == 1
        weight = jnp.concatenate(
            [jnp.where(is_root, -own_inv, weight[:half]), weight[half:]], axis=0
        )
        begin = jnp.concatenate([jnp.where(is_root, 0.0, begin[:half]), begin[half:]], axis=0)
        top_out[...] = jnp.concatenate(
            [jnp.where(is_root, own_fac, solved[:half]), solved[half:]], axis=0
        )
        moved = begin - jnp.dot(weight, starts[...], precision=HI, preferred_element_type=F32)
        w_hi, w_lo = split(-weight)
        z_hi, z_lo = split(moved)
        parts = [p[:, :top] for p in (w_hi, w_lo, w_hi, z_hi, z_lo)]
        parts.append(jnp.zeros((moved.shape[0], lhs.shape[1] - 5 * top), BF16))
        lhs[...] = jnp.concatenate(parts, axis=1)

    groups = mine.shape[0]
    for g in range(groups):
        w = width // groups
        cols = slice(g * w, (g + 1) * w)
        m, o = mine[g], other[g]
        panel = jnp.concatenate([jnp.where(core == 0, m, o), jnp.where(core == 0, o, m)], axis=0)
        where_to = jnp.concatenate([dest[:top, :]] * (w // LANES), axis=1)
        place = base + step * width + g * w + iota((top, w), 1)
        hot = jnp.where(where_to == place, 1.0, 0.0)
        keep = 1.0 - jnp.sum(hot, axis=0, keepdims=True)
        p_hi, p_lo = split(panel * keep)
        hot = hot.astype(BF16)
        fill = jnp.zeros((lhs.shape[1] - 5 * top, w), BF16)
        rhs = jnp.concatenate([p_hi, p_hi, p_lo, hot, hot, fill], axis=0)
        acc = jnp.dot(lhs[...], rhs, preferred_element_type=F32)
        keep_root = jnp.where(root == 1, 0.0, keep)
        out[:half, cols] = block[:half, cols] * keep_root + acc[:half]
        out[half:, cols] = block[half:, cols] * keep + acc[half:]

    @pl.when((step == 0) & (base == 0))
    def _():
        lanes = iota((block.shape[0], LANES), 1)
        out[:, :LANES] = jnp.where(lanes < top, top_out[...], out[:, :LANES])


def on_device(matrix, pivots):
    blocks, _, half, rows = matrix.shape
    cols = blocks * half
    top = 2 * half
    plane = ("y", "x")
    chips = lax.axis_size("y") * lax.axis_size("x")
    depth = lax.axis_size("prow")
    width = rows // chips
    holdings = matrix.reshape(cols, rows)
    core = lax.axis_index("core").astype(jnp.int32)
    base = (lax.axis_index("prow") * rows).astype(jnp.int32)
    root = ((lax.axis_index("y") == 0) & (lax.axis_index("x") == 0)).astype(jnp.int32)
    base1 = base.reshape(1)
    swap = [(0, 1), (1, 0)]

    def call(kernel, name, us, out_shape, in_specs, out_specs, *args, **more):
        return pl.pallas_call(
            lambda *refs: kernel(top, *refs),
            out_shape=out_shape,
            in_specs=in_specs,
            out_specs=out_specs,
            compiler_params=params(),
            cost_estimate=cost(us),
            name=name,
            **more,
        )(*args)

    span_x, span_y = lax.axis_size("x"), lax.axis_size("y")
    send = jax.ShapeDtypeStruct((span_y + 1, half, width), F32)
    *sends, wanted, owned, dest = call(
        start_kernel,
        "start",
        5,
        (
            *[send] * span_x,
            jax.ShapeDtypeStruct((top,), jnp.int32),
            jax.ShapeDtypeStruct((top + 8,), jnp.int32),
            jax.ShapeDtypeStruct((LANES, LANES), jnp.int32),
        ),
        [smem_spec(), smem_spec(), pl.BlockSpec((half, rows), lambda i: (0, 0))],
        (*[vmem_spec()] * span_x, smem_spec(), smem_spec(), vmem_spec()),
        pivots,
        base1,
        holdings,
        grid=(1,),
        scratch_shapes=[
            pltpu.SMEM((rows * depth,), jnp.int32),
            pltpu.SMEM((top + 8,), jnp.int32),
            pltpu.VMEM((half, LANES), F32),
        ],
    )
    along_x = [lax.ppermute(sends[k], plane, [(0, k)]) for k in range(1, span_x)]
    offered = call(
        own_kernel,
        "own",
        5,
        jax.ShapeDtypeStruct((cols, 2 * LANES), F32),
        [smem_spec()] * 3 + [pl.BlockSpec((cols, rows // 2), lambda i: (0, i))],
        pl.BlockSpec((cols, 2 * LANES), lambda i: (0, 0)),
        base1,
        wanted,
        owned,
        holdings,
        grid=(2,),
    )
    relayed = call(
        relay_kernel,
        "relay",
        1,
        send,
        [smem_spec()] + [vmem_spec()] * span_x,
        vmem_spec(),
        root.reshape(1),
        sends[0],
        *along_x,
    )
    offered, relayed = lax.optimization_barrier((offered, relayed))
    along_y = [
        lax.ppermute(relayed, plane, [(x, k * span_x + x) for x in range(span_x)])
        for k in range(1, span_y)
    ]
    share, panel_top = call(
        arrive_kernel,
        "arrive",
        0.5,
        (jax.ShapeDtypeStruct((span_y, half, width), F32), jax.ShapeDtypeStruct((half, width), F32)),
        [vmem_spec()] * span_y,
        (vmem_spec(), vmem_spec()),
        relayed,
        *along_y,
    )

    part = cols // depth
    pieces = lax.all_to_all(offered.reshape(depth, part, 2 * LANES), "prow", 0, 0)
    packed = call(
        gather_kernel,
        "gather",
        1,
        jax.ShapeDtypeStruct((depth, part, 3 * LANES), F32),
        [vmem_spec(), vmem_spec()],
        vmem_spec(),
        pieces,
        panel_top,
    )
    packed, share = lax.optimization_barrier((packed, share))
    found = [share]
    for k in range(1, span_x):
        moves = [(i, (i + k) % span_x) for i in range(span_x)]
        found.append(lax.ppermute(share, "x", moves))
    mine = call(
        order_kernel,
        "order",
        0.7,
        jax.ShapeDtypeStruct((chips, half, width), F32),
        [smem_spec()] + [vmem_spec()] * span_x,
        vmem_spec(),
        lax.axis_index("x").astype(jnp.int32).reshape(1),
        *found,
    )
    heads, square = call(
        heads_kernel,
        "heads",
        1,
        (
            jax.ShapeDtypeStruct((cols, 2 * LANES), F32),
            jax.ShapeDtypeStruct((half, 2 * LANES), F32),
        ),
        [vmem_spec()],
        (vmem_spec(), vmem_spec()),
        lax.all_to_all(packed, "prow", 0, 0),
    )
    square_other = lax.ppermute(square, "core", swap)
    mine, square_other = lax.optimization_barrier((mine, square_other))
    other = lax.ppermute(mine, "core", swap)
    small = jax.ShapeDtypeStruct((LANES, LANES), F32)
    factor, lower_inv, upper_inv, starts = pl.pallas_call(
        factor_kernel,
        out_shape=(small,) * 4,
        in_specs=[smem_spec(), vmem_spec(), vmem_spec()],
        out_specs=(vmem_spec(),) * 4,
        compiler_params=params(),
        cost_estimate=cost(9),
        name="factor",
    )(core.reshape(1), square, square_other)
    flags = jnp.stack([core, root, base])
    per_step = 8
    span = per_step * width
    whole = pl.BlockSpec((LANES, LANES), lambda i: (0, 0))
    parts = pl.BlockSpec((per_step, half, width), lambda i: (i, 0, 0))
    result = pl.pallas_call(
        lambda *refs: update_kernel(top, *refs),
        grid=(rows // span,),
        out_shape=jax.ShapeDtypeStruct((cols, rows), F32),
        in_specs=[
            smem_spec(),
            pl.BlockSpec((cols, 2 * LANES), lambda i: (0, 0)),
            whole,
            whole,
            whole,
            whole,
            whole,
            pl.BlockSpec((cols, span), lambda i: (0, i)),
            parts,
            parts,
        ],
        out_specs=pl.BlockSpec((cols, span), lambda i: (0, i)),
        scratch_shapes=[
            pltpu.VMEM((cols, 4 * LANES), BF16),
            pltpu.VMEM((cols, LANES), F32),
        ],
        compiler_params=params(),
        cost_estimate=cost(8),
        name="update",
    )(flags, heads, factor, lower_inv, upper_inv, starts, dest, holdings, mine, other)
    return result.reshape(matrix.shape)


def solution(mesh):
    fine = Mesh(mesh.devices.reshape(4, 4, 2, 8), ("y", "x", "core", "prow"))
    spec = P(None, ("y", "x", "core"), None, "prow")
    return jax.shard_map(
        on_device, mesh=fine, in_specs=(spec, P()), out_specs=spec, check_vma=False
    )
```

```python
import jax
import jax.numpy as jnp
from jax import lax
from jax.experimental import pallas as pl
from jax.experimental.pallas import tpu as pltpu
from jax.sharding import Mesh
from jax.sharding import PartitionSpec as P

HI = lax.Precision.HIGHEST
LANES = 128
F32 = jnp.float32
BF16 = jnp.bfloat16


def iota(shape, dim):
    return lax.broadcasted_iota(jnp.int32, shape, dim)


def vmem_spec():
    return pl.BlockSpec(memory_space=pltpu.VMEM)


def smem_spec():
    return pl.BlockSpec(memory_space=pltpu.SMEM)


def params(mib=48):
    return pltpu.CompilerParams(vmem_limit_bytes=mib * 1024 * 1024)


def cost(us):
    return pl.CostEstimate(flops=0, bytes_accessed=int(us * 3.5e6), transcendentals=0)


def pick_rows(wanted, owned, base, block, out):
    lanes = iota((block.shape[0], LANES), 1)

    def step(n, carry):
        i = owned[n]
        local = wanted[i] - base

        @pl.when((local >= 0) & (local < block.shape[1]))
        def _():
            start = pl.multiple_of((local // LANES) * LANES, LANES)
            shift = (i + LANES - local % LANES) % LANES
            moved = pltpu.roll(block[:, pl.ds(start, LANES)], shift, 1)
            out[:, :LANES] = jnp.where(lanes == i, moved, out[:, :LANES])

        return carry

    lax.fori_loop(0, owned[owned.shape[0] - 8], step, 0)


def start_kernel(top, pivots, base, panel, *refs):
    sends, (wanted, owned, dest, current, goes, picked) = refs[:-6], refs[-6:]
    rows = panel.shape[1]
    span = len(sends)
    width = sends[0].shape[2]

    def fill(j, carry):
        current[pivots[j]] = pivots[j]
        goes[j] = -1
        return carry

    def fill_top(j, carry):
        current[j] = j
        return carry

    def swap(j, carry):
        t = pivots[j]
        a = current[j]
        b = current[t]
        wanted[j] = b
        current[t] = a
        goes[jnp.minimum(b, top)] = -1
        goes[a] = jnp.where(t >= top, t, -1)
        owned[carry] = j
        local = b - base[0]
        return carry + ((local >= 0) & (local < rows)).astype(jnp.int32)

    def emit(j, carry):
        dest[pl.ds(j, 1), :] = jnp.full((1, LANES), goes[j], jnp.int32)
        return carry

    lax.fori_loop(0, top, fill, 0, unroll=8)
    lax.fori_loop(0, top, fill_top, 0, unroll=8)
    owned[top] = lax.fori_loop(0, top, swap, 0, unroll=8)
    dest[...] = jnp.full(dest.shape, -1, jnp.int32)
    lax.fori_loop(0, top, emit, 0, unroll=8)
    picked[...] = jnp.zeros(picked.shape, F32)
    pick_rows(wanted, owned, base[0], panel, picked)
    lanes = iota(picked.shape, 1)
    heads = jnp.where((base[0] == 0) & (lanes < top), panel[:, :LANES], 0.0)
    for x, send in enumerate(sends):
        high = send.shape[0] - 1
        for y in range(high):
            g = y * span + x
            send[y] = panel[:, g * width : (g + 1) * width]
        send[high, :, :LANES] = picked[...]
        send[high, :, LANES:] = heads


def relay_kernel(top, root, kept, *refs):
    del top
    others, out = refs[:-1], refs[-1]
    for n in range(out.shape[0]):
        total = jnp.where(root[0] == 1, kept[n], 0.0)
        for other in others:
            total = total + other[n]
        out[n] = total


def own_kernel(top, base, wanted, owned, block, out):
    step = pl.program_id(0)

    @pl.when(step == 0)
    def _():
        lanes = iota((block.shape[0], LANES), 1)
        out[:, :LANES] = jnp.zeros(lanes.shape, F32)
        out[:, LANES:] = jnp.where((base[0] == 0) & (lanes < top), block[:, :LANES], 0.0)

    pick_rows(wanted, owned, base[0] + step * block.shape[1], block, out)


def arrive_kernel(top, *refs):
    del top
    arrivals, (share, square) = refs[:-2], refs[-2:]
    count = share.shape[0]
    for n in range(count + 1):
        total = arrivals[0][n]
        for arrival in arrivals[1:]:
            total = total + arrival[n]
        if n < count:
            share[n] = total
        else:
            square[...] = total


def order_kernel(top, place, *refs):
    del top
    pieces, out = refs[:-1], refs[-1]
    span = len(pieces)
    for k, piece in enumerate(pieces):
        owner = (place[0] + span - k) % span
        for n in range(piece.shape[0]):
            out[n * span + owner] = piece[n]


def gather_kernel(top, pieces, panel_top, packed):
    depth = pieces.shape[0]
    square, begin = panel_top[:, :LANES], panel_top[:, LANES:]
    total = pieces[0]
    for z in range(1, depth):
        total = total + pieces[z]
    third = LANES - top
    tail = iota(square.shape, 1) >= top
    for n, body in enumerate((total[:, :LANES], total[:, LANES:], square)):
        moved = pltpu.roll(begin, top - n * third, 1)
        value = jnp.where(tail, moved, body)
        for z in range(depth):
            packed[z, :, n * LANES : (n + 1) * LANES] = value


def heads_kernel(top, pieces, heads, square):
    depth, part, _ = pieces.shape
    third = LANES - top
    lanes = iota((part, LANES), 1)
    total = pieces[0]
    for z in range(1, depth):
        total = total + pieces[z]
    square[:, :LANES] = jnp.where(lanes < top, total[:, 2 * LANES :], 0.0)
    begin = jnp.zeros((part, LANES), F32)
    for n in range(3):
        moved = pltpu.roll(total[:, n * LANES : (n + 1) * LANES], LANES - top + n * third, 1)
        begin = jnp.where((lanes >= n * third) & (lanes < (n + 1) * third), moved, begin)
    square[:, LANES:] = begin
    keep = iota((part, 2 * LANES), 1) % LANES < top
    for z in range(depth):
        heads[z * part : (z + 1) * part, :] = jnp.where(keep, pieces[z, :, : 2 * LANES], 0.0)


def spread(tile, j):
    return jnp.broadcast_to(tile[:, j : j + 1], (8, LANES))


def spread_row(tile, i):
    return jnp.broadcast_to(tile[i : i + 1, :], (8, LANES))


def reciprocal(x):
    r = pl.reciprocal(x, approx=True)
    r = r * (2.0 - x * r)
    return r * (2.0 - x * r)


def factor_kernel(core, mine, other, factor, lower_inv, upper_inv, starts):
    half = mine.shape[0]
    extent = 2 * half
    first = core[0] == 0
    m = mine[...]
    o = other[...]
    lo = jnp.where(first, m, o)
    hi = jnp.where(first, o, m)
    starts[:half, :] = lo[:, LANES:]
    starts[half:extent, :] = hi[:, LANES:]
    rest = jnp.zeros((LANES - extent, LANES), F32)
    starts[extent:, :] = rest
    tiles = [lo[8 * t : 8 * t + 8, :LANES] for t in range(half // 8)]
    tiles += [hi[8 * t : 8 * t + 8, :LANES] for t in range(half // 8)]
    square = jnp.concatenate(tiles + [rest], axis=0)
    lanes = iota((8, LANES), 1)
    subs = iota((8, LANES), 0)
    ahead = 5
    window = [[spread(t, q) for t in tiles] for q in range(ahead)]
    for j in range(extent):
        tj, sj = j // 8, j % 8
        here = lanes == j
        right = lanes > j
        cols = window.pop(0)
        if j + ahead < extent:
            window.append([spread(t, j + ahead) for t in tiles])
        row = spread_row(tiles[tj], sj)
        recip = reciprocal(spread_row(cols[tj], sj))
        scaled = jnp.where(here, recip, row * recip)
        right_part = jnp.where(right, scaled, 0.0)
        factor[j : j + 1, :] = right_part[:1]
        for q, nxt in enumerate(window):
            gain = spread_row(nxt[tj], sj) * recip
            moved = []
            for t, (n, col) in enumerate(zip(nxt, cols)):
                after = n - col * gain
                if t == tj:
                    after = jnp.where(subs == sj, -gain, after)
                moved.append(after)
            window[q] = moved
        new = []
        for t, (tile, col) in enumerate(zip(tiles, cols)):
            if t < tj:
                new.append(tile - col * right_part)
                continue
            below = jnp.where(here, 0.0, tile) - col * scaled
            if t == tj:
                above = tile - col * right_part
                at = jnp.where(right, -scaled, scaled)
                below = jnp.where(subs < sj, above, jnp.where(subs == sj, at, below))
            new.append(below)
        tiles = new
    for t, tile in enumerate(tiles):
        rows = subs + 8 * t
        at = pl.ds(8 * t, 8)
        lower_inv[at, :] = jnp.where(
            lanes > rows, jnp.where(lanes < extent, tile, 0.0), jnp.where(lanes == rows, 1.0, 0.0)
        )
        upper_inv[at, :] = jnp.where(lanes <= rows, tile, 0.0)
    factor[extent:, :] = rest
    lower_inv[extent:, :] = rest
    upper_inv[extent:, :] = rest
    upper = jnp.dot(square, lower_inv[...], precision=HI, preferred_element_type=F32)
    for t in range(extent // 8):
        at = pl.ds(8 * t, 8)
        rows = subs + 8 * t
        factor[at, :] = jnp.where(lanes > rows, factor[at, :], upper[8 * t : 8 * t + 8])


def split(x):
    head = x.astype(BF16)
    return head, (x - head.astype(F32)).astype(BF16)


def update_kernel(
    top, flags, heads, factor, lower_inv, upper_inv, starts, dest, block, mine, other, out,
    lhs, top_out,
):
    step = pl.program_id(0)
    half = mine.shape[1]
    width = block.shape[1]
    core, root, base = flags[0], flags[1], flags[2]

    @pl.when(step == 0)
    def _():
        tops = heads[:, :LANES]
        solved = jnp.dot(tops, lower_inv[...], precision=HI, preferred_element_type=F32)
        weight = jnp.dot(solved, upper_inv[...], precision=HI, preferred_element_type=F32)
        own_inv = jnp.where(core == 0, upper_inv[:half, :], upper_inv[half : 2 * half, :])
        own_fac = jnp.where(core == 0, factor[:half, :], factor[half : 2 * half, :])
        begin = heads[:, LANES:]
        is_root = root == 1
        weight = jnp.concatenate(
            [jnp.where(is_root, -own_inv, weight[:half]), weight[half:]], axis=0
        )
        begin = jnp.concatenate([jnp.where(is_root, 0.0, begin[:half]), begin[half:]], axis=0)
        top_out[...] = jnp.concatenate(
            [jnp.where(is_root, own_fac, solved[:half]), solved[half:]], axis=0
        )
        moved = begin - jnp.dot(weight, starts[...], precision=HI, preferred_element_type=F32)
        w_hi, w_lo = split(-weight)
        z_hi, z_lo = split(moved)
        parts = [p[:, :top] for p in (w_hi, w_lo, w_hi, z_hi, z_lo)]
        parts.append(jnp.zeros((moved.shape[0], lhs.shape[1] - 5 * top), BF16))
        lhs[...] = jnp.concatenate(parts, axis=1)

    groups = mine.shape[0]
    for g in range(groups):
        w = width // groups
        cols = slice(g * w, (g + 1) * w)
        m, o = mine[g], other[g]
        panel = jnp.concatenate([jnp.where(core == 0, m, o), jnp.where(core == 0, o, m)], axis=0)
        where_to = jnp.concatenate([dest[:top, :]] * (w // LANES), axis=1)
        place = base + step * width + g * w + iota((top, w), 1)
        hot = jnp.where(where_to == place, 1.0, 0.0)
        keep = 1.0 - jnp.sum(hot, axis=0, keepdims=True)
        p_hi, p_lo = split(panel * keep)
        hot = hot.astype(BF16)
        fill = jnp.zeros((lhs.shape[1] - 5 * top, w), BF16)
        rhs = jnp.concatenate([p_hi, p_hi, p_lo, hot, hot, fill], axis=0)
        acc = jnp.dot(lhs[...], rhs, preferred_element_type=F32)
        keep_root = jnp.where(root == 1, 0.0, keep)
        out[:half, cols] = block[:half, cols] * keep_root + acc[:half]
        out[half:, cols] = block[half:, cols] * keep + acc[half:]

    @pl.when((step == 0) & (base == 0))
    def _():
        lanes = iota((block.shape[0], LANES), 1)
        out[:, :LANES] = jnp.where(lanes < top, top_out[...], out[:, :LANES])


def on_device(matrix, pivots):
    blocks, _, half, rows = matrix.shape
    cols = blocks * half
    top = 2 * half
    plane = ("y", "x")
    chips = lax.axis_size("y") * lax.axis_size("x")
    depth = lax.axis_size("prow")
    width = rows // chips
    holdings = matrix.reshape(cols, rows)
    core = lax.axis_index("core").astype(jnp.int32)
    base = (lax.axis_index("prow") * rows).astype(jnp.int32)
    root = ((lax.axis_index("y") == 0) & (lax.axis_index("x") == 0)).astype(jnp.int32)
    base1 = base.reshape(1)
    swap = [(0, 1), (1, 0)]

    def call(kernel, name, us, out_shape, in_specs, out_specs, *args, **more):
        return pl.pallas_call(
            lambda *refs: kernel(top, *refs),
            out_shape=out_shape,
            in_specs=in_specs,
            out_specs=out_specs,
            compiler_params=params(),
            cost_estimate=cost(us),
            name=name,
            **more,
        )(*args)

    span_x, span_y = lax.axis_size("x"), lax.axis_size("y")
    send = jax.ShapeDtypeStruct((span_y + 1, half, width), F32)
    *sends, wanted, owned, dest = call(
        start_kernel,
        "start",
        5,
        (
            *[send] * span_x,
            jax.ShapeDtypeStruct((top,), jnp.int32),
            jax.ShapeDtypeStruct((top + 8,), jnp.int32),
            jax.ShapeDtypeStruct((LANES, LANES), jnp.int32),
        ),
        [smem_spec(), smem_spec(), pl.BlockSpec((half, rows), lambda i: (0, 0))],
        (*[vmem_spec()] * span_x, smem_spec(), smem_spec(), vmem_spec()),
        pivots,
        base1,
        holdings,
        grid=(1,),
        scratch_shapes=[
            pltpu.SMEM((rows * depth,), jnp.int32),
            pltpu.SMEM((top + 8,), jnp.int32),
            pltpu.VMEM((half, LANES), F32),
        ],
    )
    along_x = [lax.ppermute(sends[k], plane, [(0, k)]) for k in range(1, span_x)]
    offered = call(
        own_kernel,
        "own",
        5,
        jax.ShapeDtypeStruct((cols, 2 * LANES), F32),
        [smem_spec()] * 3 + [pl.BlockSpec((cols, rows // 2), lambda i: (0, i))],
        pl.BlockSpec((cols, 2 * LANES), lambda i: (0, 0)),
        base1,
        wanted,
        owned,
        holdings,
        grid=(2,),
    )
    relayed = call(
        relay_kernel,
        "relay",
        1,
        send,
        [smem_spec()] + [vmem_spec()] * span_x,
        vmem_spec(),
        root.reshape(1),
        sends[0],
        *along_x,
    )
    offered, relayed = lax.optimization_barrier((offered, relayed))
    along_y = [
        lax.ppermute(relayed, plane, [(x, k * span_x + x) for x in range(span_x)])
        for k in range(1, span_y)
    ]
    share, panel_top = call(
        arrive_kernel,
        "arrive",
        0.5,
        (jax.ShapeDtypeStruct((span_y, half, width), F32), jax.ShapeDtypeStruct((half, width), F32)),
        [vmem_spec()] * span_y,
        (vmem_spec(), vmem_spec()),
        relayed,
        *along_y,
    )

    part = cols // depth
    pieces = lax.all_to_all(offered.reshape(depth, part, 2 * LANES), "prow", 0, 0)
    packed = call(
        gather_kernel,
        "gather",
        1,
        jax.ShapeDtypeStruct((depth, part, 3 * LANES), F32),
        [vmem_spec(), vmem_spec()],
        vmem_spec(),
        pieces,
        panel_top,
    )
    packed, share = lax.optimization_barrier((packed, share))
    found = [share]
    for k in range(1, span_x):
        moves = [(i, (i + k) % span_x) for i in range(span_x)]
        found.append(lax.ppermute(share, "x", moves))
    mine = call(
        order_kernel,
        "order",
        0.7,
        jax.ShapeDtypeStruct((chips, half, width), F32),
        [smem_spec()] + [vmem_spec()] * span_x,
        vmem_spec(),
        lax.axis_index("x").astype(jnp.int32).reshape(1),
        *found,
    )
    heads, square = call(
        heads_kernel,
        "heads",
        1,
        (
            jax.ShapeDtypeStruct((cols, 2 * LANES), F32),
            jax.ShapeDtypeStruct((half, 2 * LANES), F32),
        ),
        [vmem_spec()],
        (vmem_spec(), vmem_spec()),
        lax.all_to_all(packed, "prow", 0, 0),
    )
    square_other = lax.ppermute(square, "core", swap)
    mine, square_other = lax.optimization_barrier((mine, square_other))
    other = lax.ppermute(mine, "core", swap)
    small = jax.ShapeDtypeStruct((LANES, LANES), F32)
    factor, lower_inv, upper_inv, starts = pl.pallas_call(
        factor_kernel,
        out_shape=(small,) * 4,
        in_specs=[smem_spec(), vmem_spec(), vmem_spec()],
        out_specs=(vmem_spec(),) * 4,
        compiler_params=params(),
        cost_estimate=cost(9),
        name="factor",
    )(core.reshape(1), square, square_other)
    flags = jnp.stack([core, root, base])
    per_step = 8
    span = per_step * width
    whole = pl.BlockSpec((LANES, LANES), lambda i: (0, 0))
    parts = pl.BlockSpec((per_step, half, width), lambda i: (i, 0, 0))
    result = pl.pallas_call(
        lambda *refs: update_kernel(top, *refs),
        grid=(rows // span,),
        out_shape=jax.ShapeDtypeStruct((cols, rows), F32),
        in_specs=[
            smem_spec(),
            pl.BlockSpec((cols, 2 * LANES), lambda i: (0, 0)),
            whole,
            whole,
            whole,
            whole,
            whole,
            pl.BlockSpec((cols, span), lambda i: (0, i)),
            parts,
            parts,
        ],
        out_specs=pl.BlockSpec((cols, span), lambda i: (0, i)),
        scratch_shapes=[
            pltpu.VMEM((cols, 4 * LANES), BF16),
            pltpu.VMEM((cols, LANES), F32),
        ],
        compiler_params=params(),
        cost_estimate=cost(8),
        name="update",
    )(flags, heads, factor, lower_inv, upper_inv, starts, dest, holdings, mine, other)
    return result.reshape(matrix.shape)


def solution(mesh):
    fine = Mesh(mesh.devices.reshape(4, 4, 2, 8), ("y", "x", "core", "prow"))
    spec = P(None, ("y", "x", "core"), None, "prow")
    return jax.shard_map(
        on_device, mesh=fine, in_specs=(spec, P()), out_specs=spec, check_vma=False
    )
```
